32 devices in a mesh: groups: 2 (over y), row: 4 (over x, core), col: 4 (over z).
Axes of the slice: x: 2, y: 2, z: 4, core: 2. Of those that a mesh axis runs over, the one named last changes fastest.
Arguments:
- adjacency: bfloat16 [8, 4, 32, 128, 128], P(('groups', 'row'), 'col'), parts along dimension 0, may hold values from 0.049804688 to 1
- tile_row: int32 [8, 4, 32], P(('groups', 'row'), 'col'), parts along dimension 0, may hold values from -1 to 7, as said below
- tile_col: int32 [8, 4, 32], P(('groups', 'row'), 'col'), parts along dimension 0, may hold values from -1 to 7, as said below
- seed_node: int32 [512], P('groups'), parts along dimension 0, may hold values from 0 to 4095
- teleport_block: int32 [512], P('groups'), parts along dimension 0, may hold values from 0 to 31
- previous: float32 [8192, 256], P(('groups', 'row', 'col')), parts along dimension 0, may hold values from 0.1 to 10
Outputs:
- rank_field: float32 [8192, 256], P(('groups', 'row', 'col')), parts along dimension 0
The draws below stay inside these ranges and needn't reach their ends.
There are 2 independent parts, one for each index of `groups`. The reference program is written for one: setup_inputs(seed, part) draws one part's arguments, and reference() takes and returns one part's arrays. A program takes and returns all parts, laid end to end along the dimension named above; each array names one. Nothing has to cross between parts.
Inputs may be any that keep to these rules, and one draw needn't show every extreme that they name: On each device the slots with entries >= 0 come first, and tile_row and tile_col are -1 together on the other slots; a device's (tile_row, tile_col) pairs are distinct; in every part exactly one device has all 32 slots used and every other device uses between 5 and 10 of them. `tile_col`: empty exactly where tile_row is empty. In every part, for each index of row, at least one tile column holds no tile on any device with that index of row.
All inputs are finite; a program needn't handle non-finite values.
Results may differ from the reference program's by a relative error of at most 0.0003.
Values may be sent and summed in bfloat16 or wider, within the bound.
A program may use at most 64 MiB of HBM per device.

```python
import math
import jax
import jax.numpy as jnp
from jax import lax

OWNED = 256
SEEDS = 256
TILE = 128
ITERS = 3
NODES = 4096
TILE_SLOTS = 32
N_ROW = 4
N_COL = 4


def tile_layout(key):
    device_count = N_ROW * N_COL
    tile_rows = OWNED * N_ROW // TILE
    tile_cols = OWNED * N_COL // TILE
    usable_cols = tile_cols - 1
    base_key = jax.random.fold_in(key, 7)
    counts = jax.random.randint(jax.random.fold_in(base_key, 1), (device_count,), TILE_SLOTS // 6, TILE_SLOTS // 3 + 1)
    heaviest = jax.random.randint(jax.random.fold_in(base_key, 2), (), 0, device_count)
    counts = jnp.where(jnp.arange(device_count) == heaviest, TILE_SLOTS, counts)
    empty_cols = jax.random.randint(jax.random.fold_in(base_key, 4), (N_ROW,), 0, tile_cols)
    device_empty = jnp.repeat(empty_cols, N_COL)
    device_keys = jax.random.split(jax.random.fold_in(base_key, 3), device_count)

    def choose_places(device_key):
        return jax.random.permutation(device_key, tile_rows * usable_cols)[:TILE_SLOTS]
    places = jax.vmap(choose_places)(device_keys)
    narrow_cols = places % usable_cols
    full_cols = narrow_cols + (narrow_cols >= device_empty[:, None]).astype(jnp.int32)
    used_slot = jnp.arange(TILE_SLOTS)[None, :] < counts[:, None]
    rows_out = jnp.where(used_slot, places // usable_cols, -1).astype(jnp.int32)
    cols_out = jnp.where(used_slot, full_cols, -1).astype(jnp.int32)
    return (rows_out.reshape(N_ROW, N_COL, TILE_SLOTS), cols_out.reshape(N_ROW, N_COL, TILE_SLOTS))


def draw_tile_row(key, part):
    return tile_layout(key)[0]


def draw_tile_col(key, part):
    return tile_layout(key)[1]


def plant(values, key, least, top_value):
    longest = values.shape.index(max(values.shape))
    spots = []
    for shift in (0, 1):
        where = [jax.random.randint(jax.random.fold_in(key, axis), (), 0, length) for axis, length in enumerate(values.shape)]
        where[longest] = (where[longest] + shift) % values.shape[longest]
        spots.append(tuple(where))
    return values.at[spots[0]].set(least).at[spots[1]].set(top_value)


def block_scale(rng, shape, shards, smallest, largest):
    factor_of, own = 1.0, jax.random.fold_in(rng, 6)
    for position, shards_of in shards:
        heights = jnp.exp(jax.random.uniform(jax.random.fold_in(own, position), (shards_of,), jnp.float32, smallest / len(shards), largest / len(shards)))
        factor_of = factor_of * jnp.repeat(heights, shape[position] // shards_of).reshape([-1 if axis == position else 1 for axis in range(len(shape))])
    return factor_of


def setup_inputs(seed: int = 0, part: int = 0) -> dict:
    keys = jax.random.split(jax.random.key(seed), 7)
    part_keys = jax.random.split(jax.random.fold_in(keys[6], part), 7)
    return {
        "adjacency": jnp.clip(0.049804688 + 0.9501953 * jax.random.uniform(part_keys[0], (N_ROW, N_COL, TILE_SLOTS, TILE, TILE), jnp.float32) ** block_scale(part_keys[0], (N_ROW, N_COL, TILE_SLOTS, TILE, TILE), ((0, 4), (1, 4)), -0.2, 0.2), 0.049804688, 1.0).astype(jnp.bfloat16),
        "tile_row": draw_tile_row(jax.random.fold_in(jax.random.fold_in(keys[6], part), 71), part),
        "tile_col": draw_tile_col(jax.random.fold_in(jax.random.fold_in(keys[6], part), 71), part),
        "seed_node": plant(jax.random.randint(part_keys[3], (SEEDS,), 0, NODES), jax.random.fold_in(part_keys[3], 1), 0, NODES - 1).astype(jnp.int32),
        "teleport_block": plant(jax.random.randint(part_keys[4], (SEEDS,), 0, NODES // TILE), jax.random.fold_in(part_keys[4], 1), 0, (NODES // TILE) - 1).astype(jnp.int32),
        "previous": jnp.clip(jnp.exp(math.log(10.0) - 4.6051702 * jax.random.uniform(part_keys[5], (NODES, SEEDS), jnp.float32) ** block_scale(part_keys[5], (NODES, SEEDS), ((0, 16),), -0.2, 0.2)), 0.1, 10.0),
    }


damping = 0.85
highest = lax.Precision.HIGHEST


def teleport_weights(node_ids, seed_node, teleport_block):
    at_seed = (node_ids[:, None] == seed_node[None, :]).astype(jnp.float32)
    in_block = ((node_ids // TILE)[:, None] == teleport_block[None, :]).astype(jnp.float32)
    return 4.0 * at_seed + 2.0 * in_block


def reference(adjacency, tile_row, tile_col, seed_node, teleport_block, previous):
    tile_rows = OWNED * N_ROW // TILE
    tile_cols = OWNED * N_COL // TILE
    device_count = N_ROW * N_COL
    column_sums = jnp.sum(adjacency.astype(jnp.float32), axis=3)
    col_place = (tile_col[..., None] == jnp.arange(tile_cols, dtype=jnp.int32)).astype(jnp.float32)
    degree = jnp.einsum('rctj,rctb->rjb', col_place, column_sums, precision=highest)
    divisor = jnp.maximum(degree.reshape(N_ROW, tile_cols * TILE), 1.0)
    teleport = teleport_weights(jnp.arange(NODES, dtype=jnp.int32), seed_node, teleport_block)
    flat_tiles = adjacency.reshape(device_count, TILE_SLOTS, TILE, TILE)
    flat_rows = tile_row.reshape(device_count, TILE_SLOTS)
    flat_cols = tile_col.reshape(device_count, TILE_SLOTS)
    rank_field = previous
    for iteration in range(ITERS):
        scaled = rank_field.reshape(N_ROW, N_COL * OWNED, SEEDS) / divisor[:, :, None]
        panels = scaled.astype(jnp.bfloat16).reshape(N_ROW, tile_cols, TILE, SEEDS)

        def device_term(device_index):
            source_panel = panels[device_index // N_COL]
            picked = jnp.take(source_panel, jnp.maximum(flat_cols[device_index], 0), axis=0).astype(jnp.float32)
            products = jnp.einsum('tab,tbs->tas', flat_tiles[device_index].astype(jnp.float32), picked, precision=highest)
            placing = (flat_rows[device_index][:, None] == jnp.arange(tile_rows, dtype=jnp.int32)[None, :]).astype(jnp.float32)
            gathered = jnp.einsum('ti,tas->ias', placing, products, precision=highest)
            return gathered.reshape(N_ROW, OWNED, SEEDS)

        partials = lax.map(device_term, jnp.arange(device_count, dtype=jnp.int32))
        summed = jnp.sum(partials.reshape(N_ROW, N_COL, N_ROW, OWNED, SEEDS), axis=0)
        summed = jnp.transpose(summed, (1, 0, 2, 3)).reshape(NODES, SEEDS)
        rank_field = damping * summed + (1.0 - damping) * teleport
    return rank_field
```

```python
import functools

import jax
import jax.numpy as jnp
from jax import lax
from jax.experimental import pallas as pl
from jax.experimental.pallas import tpu as pltpu
from jax.sharding import PartitionSpec as P

ITERS = 3
LANES = 128
DAMPING = 0.85
MESH = pl.DeviceIdType.MESH


def refresh_kernel(
    n_row, n_col, slot_ref, adj_ref, seed_ref, block_ref, prev_ref, out_ref,
    link, sums_out, sums_in, inverse, restart, panels, mine,
    half_out, half_in, full_out, full_in,
    sums_ss, sums_rs, col_ss, col_rs, row_ss, row_rs,
):
    r, c = lax.axis_index("row"), lax.axis_index("col")
    owned, seeds = prev_ref.shape
    edge = adj_ref.shape[1]
    targets, sources = link.shape
    tile_rows, tile_cols = targets // edge, sources // edge
    chunks = seeds // LANES

    barrier = pltpu.get_barrier_semaphore()
    for d in range(1, n_col):
        pl.semaphore_signal(barrier, 1, device_id={"col": lax.rem(c + d, n_col)}, device_id_type=MESH)
    for e in range(1, n_row):
        pl.semaphore_signal(barrier, 1, device_id={"row": lax.rem(r + e, n_row)}, device_id_type=MESH)

    @pl.loop(0, tile_rows)
    def _(i):
        for j in range(tile_cols):
            slot = slot_ref[i * tile_cols + j]
            tile = adj_ref[jnp.maximum(slot - 1, 0)]
            link[pl.ds(i * edge, edge), j * edge : (j + 1) * edge] = jnp.where(
                slot > 0, tile, jnp.zeros_like(tile)
            )

    ones = jnp.ones((16, targets), jnp.bfloat16)
    for k in range(n_col):
        columns = slice(k * owned, (k + 1) * owned)
        total = jnp.dot(ones, link[:, columns], preferred_element_type=jnp.float32)
        sums_out[k] = total[:8]

    pl.semaphore_wait(barrier, n_col - 1 + n_row - 1)

    def sums_copy(d):
        dst = lax.rem(c + d, n_col)
        return pltpu.make_async_remote_copy(
            src_ref=sums_out.at[dst], dst_ref=sums_in.at[d],
            send_sem=sums_ss.at[d], recv_sem=sums_rs.at[d],
            device_id={"col": dst}, device_id_type=MESH,
        )

    def col_copy(it, h, d):
        dst = lax.rem(c + d, n_col)
        place = panels.at[it, h, pl.ds(pl.multiple_of(c * owned, owned), owned)]
        return pltpu.make_async_remote_copy(
            src_ref=place, dst_ref=place,
            send_sem=col_ss.at[it, h, d], recv_sem=col_rs.at[it, h, d],
            device_id={"col": dst}, device_id_type=MESH,
        )

    def row_copy(it, h, e):
        last = it == ITERS - 1
        src = full_out.at[h, e] if last else half_out.at[it, h, e]
        dst = full_in.at[h, e] if last else half_in.at[it, h, e]
        return pltpu.make_async_remote_copy(
            src_ref=src, dst_ref=dst,
            send_sem=row_ss.at[it, h, e], recv_sem=row_rs.at[it, h, e],
            device_id={"row": lax.rem(r + e, n_row)}, device_id_type=MESH,
        )

    for d in range(1, n_col):
        sums_copy(d).start()

    row_of = lax.broadcasted_iota(jnp.int32, (owned, seeds), 0)
    first = (r * n_col + c) * owned
    at_seed = (row_of + first == seed_ref[...]).astype(jnp.float32)
    in_block = ((row_of + first) // edge == block_ref[...]).astype(jnp.float32)
    restart[...] = (1.0 - DAMPING) * (4.0 * at_seed + 2.0 * in_block)

    total = sums_out[c]
    for d in range(1, n_col):
        sums_copy(d).wait_recv()
        total = total + sums_in[d]
    wide = jnp.broadcast_to(1.0 / jnp.maximum(total[0:1], 1.0), (LANES, owned))
    inverse[...] = jnp.transpose(wide)

    def share(it, h, ranks):
        place = pl.ds(pl.multiple_of(c * owned, owned), owned)
        panels[it, h, place] = (ranks * inverse[...]).astype(jnp.bfloat16)
        for d in range(1, n_col):
            col_copy(it, h, d).start()

    for h in range(chunks):
        share(0, h, prev_ref[:, h * LANES : (h + 1) * LANES])

    for it in range(ITERS):
        for h in range(chunks):
            for d in range(1, n_col):
                col_copy(it, h, d).wait_recv()
            for e in list(range(1, n_row)) + [0]:
                dst = lax.rem(r + e, n_row)
                rows = pl.ds(pl.multiple_of(dst * owned, owned), owned)
                part = jnp.dot(link[rows, :], panels[it, h], preferred_element_type=jnp.float32)
                if e == 0:
                    mine[it, h] = part
                else:
                    if it == ITERS - 1:
                        full_out[h, e] = part
                    else:
                        half_out[it, h, e] = part.astype(jnp.bfloat16)
                    row_copy(it, h, e).start()
        for h in range(chunks):
            summed = mine[it, h]
            for e in range(1, n_row):
                row_copy(it, h, e).wait_recv()
                if it == ITERS - 1:
                    summed = summed + full_in[h, e]
                else:
                    summed = summed + half_in[it, h, e].astype(jnp.float32)
            lanes = slice(h * LANES, (h + 1) * LANES)
            ranks = DAMPING * summed + restart[:, lanes]
            if it == ITERS - 1:
                out_ref[:, lanes] = ranks
            else:
                share(it + 1, h, ranks)

    for d in range(1, n_col):
        sums_copy(d).wait_send()
    for it in range(ITERS):
        for h in range(chunks):
            for d in range(1, n_col):
                col_copy(it, h, d).wait_send()
            for e in range(1, n_row):
                row_copy(it, h, e).wait_send()


def on_device(adjacency, tile_row, tile_col, seed_node, teleport_block, previous):
    tiles = adjacency[0, 0]
    rows, cols = tile_row[0, 0], tile_col[0, 0]
    slots, edge = tiles.shape[:2]
    owned, seeds = previous.shape
    n_row, n_col = lax.axis_size("row"), lax.axis_size("col")
    targets, sources = n_row * owned, n_col * owned
    tile_rows, tile_cols = targets // edge, sources // edge
    chunks = seeds // LANES
    key = jnp.where(rows >= 0, rows * tile_cols + cols, -1)
    places = jnp.arange(tile_rows * tile_cols, dtype=jnp.int32)
    number = jnp.arange(1, slots + 1, dtype=jnp.int32)
    slot_of = jnp.sum(jnp.where(places[:, None] == key[None, :], number[None, :], 0), axis=1)
    vmem = pl.BlockSpec(memory_space=pltpu.VMEM)
    dma = pltpu.SemaphoreType.DMA
    return pl.pallas_call(
        functools.partial(refresh_kernel, n_row, n_col),
        out_shape=jax.ShapeDtypeStruct((owned, seeds), jnp.float32),
        in_specs=[pl.BlockSpec(memory_space=pltpu.SMEM)] + [vmem] * 4,
        out_specs=vmem,
        scratch_shapes=[
            pltpu.VMEM((targets, sources), jnp.bfloat16),
            pltpu.VMEM((n_col, 8, owned), jnp.float32),
            pltpu.VMEM((n_col, 8, owned), jnp.float32),
            pltpu.VMEM((owned, LANES), jnp.float32),
            pltpu.VMEM((owned, seeds), jnp.float32),
            pltpu.VMEM((ITERS, chunks, sources, LANES), jnp.bfloat16),
            pltpu.VMEM((ITERS, chunks, owned, LANES), jnp.float32),
            pltpu.VMEM((ITERS - 1, chunks, n_row, owned, LANES), jnp.bfloat16),
            pltpu.VMEM((ITERS - 1, chunks, n_row, owned, LANES), jnp.bfloat16),
            pltpu.VMEM((chunks, n_row, owned, LANES), jnp.float32),
            pltpu.VMEM((chunks, n_row, owned, LANES), jnp.float32),
            dma((n_col,)),
            dma((n_col,)),
            dma((ITERS, chunks, n_col)),
            dma((ITERS, chunks, n_col)),
            dma((ITERS, chunks, n_row)),
            dma((ITERS, chunks, n_row)),
        ],
        compiler_params=pltpu.CompilerParams(
            collective_id=0, has_side_effects=True, vmem_limit_bytes=56 * 2**20
        ),
    )(slot_of, tiles, seed_node[None, :], teleport_block[None, :], previous)


def solution(mesh):
    in_specs = (
        P(("groups", "row"), "col", None, None, None),
        P(("groups", "row"), "col", None),
        P(("groups", "row"), "col", None),
        P("groups"),
        P("groups"),
        P(("groups", "row", "col"), None),
    )
    out_specs = P(("groups", "row", "col"), None)
    return jax.shard_map(
        on_device, mesh=mesh, in_specs=in_specs, out_specs=out_specs, check_vma=False
    )
```

```python
import functools

import jax
import jax.numpy as jnp
from jax import lax
from jax.experimental import pallas as pl
from jax.experimental.pallas import tpu as pltpu
from jax.sharding import PartitionSpec as P

ITERS = 3
LANES = 128
DAMPING = 0.85
MESH = pl.DeviceIdType.MESH


def refresh_kernel(
    n_row, n_col, slot_ref, tiles_ref, tile_col_ref, seed_ref, block_ref, prev_ref, out_ref,
    adj_ref, adj_sem, link, sums_out, sums_in, inverse, restart, panels, kept,
    pair_out, pair_in, half_out, half_in, full_out, full_in,
    sums_ss, sums_rs, col_ss, col_rs, pair_ss, pair_rs, row_ss, row_rs,
):
    r, c = lax.axis_index("row"), lax.axis_index("col")
    owned, seeds = prev_ref.shape
    slots, edge = adj_ref.shape[:2]
    held = owned // edge
    targets, sources = link.shape
    tile_rows, tile_cols = targets // edge, sources // edge
    chunks = seeds // LANES
    chips = n_row // 2
    chip, core = r // 2, lax.rem(r, 2)
    mate = r + 1 - 2 * core

    barrier = pltpu.get_barrier_semaphore()
    for d in range(1, n_col):
        pl.semaphore_signal(barrier, 1, device_id={"col": lax.rem(c + d, n_col)}, device_id_type=MESH)
    pl.semaphore_signal(barrier, 1, device_id={"row": mate}, device_id_type=MESH)
    for e in range(1, chips):
        pl.semaphore_signal(
            barrier, 1, device_id={"row": lax.rem(chip + e, chips) * 2 + core}, device_id_type=MESH
        )

    load = pltpu.make_async_copy(tiles_ref, adj_ref, adj_sem)
    load.start()
    row_of = lax.broadcasted_iota(jnp.int32, (owned, seeds), 0)
    first = (r * n_col + c) * owned
    at_seed = (row_of + first == seed_ref[...]).astype(jnp.float32)
    in_block = ((row_of + first) // edge == block_ref[...]).astype(jnp.float32)
    restart[...] = (1.0 - DAMPING) * (4.0 * at_seed + 2.0 * in_block)
    load.wait()

    tile_sums = jnp.sum(adj_ref[...].astype(jnp.float32), axis=1)
    column_of = lax.broadcasted_iota(jnp.int32, (tile_cols, slots), 0)
    placed = (column_of == tile_col_ref[...]).astype(jnp.float32)
    sums = jnp.dot(
        placed, tile_sums, precision=lax.Precision.HIGHEST, preferred_element_type=jnp.float32
    )
    for k in range(n_col):
        sums_out[k, :held] = sums[k * held : (k + 1) * held]

    pl.semaphore_wait(barrier, n_col - 1 + chips)

    def sums_copy(d):
        dst = lax.rem(c + d, n_col)
        return pltpu.make_async_remote_copy(
            src_ref=sums_out.at[dst], dst_ref=sums_in.at[d],
            send_sem=sums_ss.at[d], recv_sem=sums_rs.at[d],
            device_id={"col": dst}, device_id_type=MESH,
        )

    def col_copy(it, h, d):
        dst = lax.rem(c + d, n_col)
        place = panels.at[it, h, pl.ds(pl.multiple_of(c * owned, owned), owned)]
        return pltpu.make_async_remote_copy(
            src_ref=place, dst_ref=place,
            send_sem=col_ss.at[it, h, d], recv_sem=col_rs.at[it, h, d],
            device_id={"col": dst}, device_id_type=MESH,
        )

    def pair_copy(it, h, e):
        return pltpu.make_async_remote_copy(
            src_ref=pair_out.at[it, h, e], dst_ref=pair_in.at[it, h, e],
            send_sem=pair_ss.at[it, h, e], recv_sem=pair_rs.at[it, h, e],
            device_id={"row": mate}, device_id_type=MESH,
        )

    def row_copy(it, h, e):
        last = it == ITERS - 1
        src = full_out.at[h, e] if last else half_out.at[it, h, e]
        dst = full_in.at[h, e] if last else half_in.at[it, h, e]
        return pltpu.make_async_remote_copy(
            src_ref=src, dst_ref=dst,
            send_sem=row_ss.at[it, h, e], recv_sem=row_rs.at[it, h, e],
            device_id={"row": lax.rem(chip + e, chips) * 2 + core}, device_id_type=MESH,
        )

    def product(it, h, e, of_core):
        dst = lax.rem(chip + e, chips) * 2 + of_core
        rows = pl.ds(pl.multiple_of(dst * owned, owned), owned)
        return jnp.dot(link[rows, :], panels[it, h], preferred_element_type=jnp.float32)

    for d in range(1, n_col):
        sums_copy(d).start()

    @pl.loop(0, tile_rows)
    def _(i):
        for j in range(tile_cols):
            slot = slot_ref[i * tile_cols + j]
            tile = adj_ref[jnp.maximum(slot - 1, 0)]
            link[pl.ds(i * edge, edge), j * edge : (j + 1) * edge] = jnp.where(
                slot > 0, tile, jnp.zeros_like(tile)
            )

    total = sums_out[c, :held]
    for d in range(1, n_col):
        sums_copy(d).wait_recv()
        total = total + sums_in[d, :held]
    scale = 1.0 / jnp.maximum(total, 1.0)
    for t in range(held):
        wide = jnp.broadcast_to(scale[t : t + 1], (LANES, edge))
        inverse[t * edge : (t + 1) * edge] = jnp.transpose(wide)

    def share(it, h, ranks):
        place = pl.ds(pl.multiple_of(c * owned, owned), owned)
        panels[it, h, place] = (ranks * inverse[...]).astype(jnp.bfloat16)
        for d in range(1, n_col):
            col_copy(it, h, d).start()

    share(0, 0, prev_ref[:, :LANES])

    for it in range(ITERS):
        for h in range(chunks):
            for d in range(1, n_col):
                col_copy(it, h, d).wait_recv()
            if it == 0 and h + 1 < chunks:
                share(0, h + 1, prev_ref[:, (h + 1) * LANES : (h + 2) * LANES])
            @pl.loop(1, chips + 1, unroll=chips <= 2)
            def _(e):
                place = lax.rem(e, chips)
                pair_out[it, h, place] = product(it, h, place, 1 - core)
                pair_copy(it, h, place).start()

            @pl.loop(1, chips + 1, unroll=chips <= 2)
            def _(e):
                place = lax.rem(e, chips)
                kept[it, h, place] = product(it, h, place, core)

            for e in range(1, chips):
                pair_copy(it, h, e).wait_recv()
                part = kept[it, h, e] + pair_in[it, h, e]
                if it == ITERS - 1:
                    full_out[h, e] = part
                else:
                    half_out[it, h, e] = part.astype(jnp.bfloat16)
                row_copy(it, h, e).start()
            pair_copy(it, h, 0).wait_recv()
            summed = kept[it, h, 0] + pair_in[it, h, 0]
            for e in range(1, chips):
                row_copy(it, h, e).wait_recv()
                if it == ITERS - 1:
                    summed = summed + full_in[h, e]
                else:
                    summed = summed + half_in[it, h, e].astype(jnp.float32)
            lanes = slice(h * LANES, (h + 1) * LANES)
            ranks = DAMPING * summed + restart[:, lanes]
            if it == ITERS - 1:
                out_ref[:, lanes] = ranks
            else:
                share(it + 1, h, ranks)

    for d in range(1, n_col):
        sums_copy(d).wait_send()
    for it in range(ITERS):
        for h in range(chunks):
            for d in range(1, n_col):
                col_copy(it, h, d).wait_send()
            for e in range(chips):
                pair_copy(it, h, e).wait_send()
            for e in range(1, chips):
                row_copy(it, h, e).wait_send()


def on_device(adjacency, tile_row, tile_col, seed_node, teleport_block, previous):
    tiles = adjacency[0, 0]
    rows, cols = tile_row[0, 0], tile_col[0, 0]
    slots, edge = tiles.shape[:2]
    owned, seeds = previous.shape
    n_row, n_col = lax.axis_size("row"), lax.axis_size("col")
    targets, sources = n_row * owned, n_col * owned
    tile_rows, tile_cols = targets // edge, sources // edge
    chunks, chips = seeds // LANES, n_row // 2
    key = jnp.where(rows >= 0, rows * tile_cols + cols, -1)
    places = jnp.arange(tile_rows * tile_cols, dtype=jnp.int32)
    number = jnp.arange(1, slots + 1, dtype=jnp.int32)
    slot_of = jnp.sum(jnp.where(places[:, None] == key[None, :], number[None, :], 0), axis=1)
    vmem = pl.BlockSpec(memory_space=pltpu.VMEM)
    dma = pltpu.SemaphoreType.DMA
    return pl.pallas_call(
        functools.partial(refresh_kernel, n_row, n_col),
        out_shape=jax.ShapeDtypeStruct((owned, seeds), jnp.float32),
        in_specs=[pl.BlockSpec(memory_space=pltpu.SMEM), pl.BlockSpec(memory_space=pl.ANY)] + [vmem] * 4,
        out_specs=vmem,
        scratch_shapes=[
            pltpu.VMEM(tiles.shape, jnp.bfloat16),
            dma,
            pltpu.VMEM((targets, sources), jnp.bfloat16),
            pltpu.VMEM((n_col, 8, edge), jnp.float32),
            pltpu.VMEM((n_col, 8, edge), jnp.float32),
            pltpu.VMEM((owned, LANES), jnp.float32),
            pltpu.VMEM((owned, seeds), jnp.float32),
            pltpu.VMEM((ITERS, chunks, sources, LANES), jnp.bfloat16),
            pltpu.VMEM((ITERS, chunks, chips, owned, LANES), jnp.float32),
            pltpu.VMEM((ITERS, chunks, chips, owned, LANES), jnp.float32),
            pltpu.VMEM((ITERS, chunks, chips, owned, LANES), jnp.float32),
            pltpu.VMEM((ITERS - 1, chunks, chips, owned, LANES), jnp.bfloat16),
            pltpu.VMEM((ITERS - 1, chunks, chips, owned, LANES), jnp.bfloat16),
            pltpu.VMEM((chunks, chips, owned, LANES), jnp.float32),
            pltpu.VMEM((chunks, chips, owned, LANES), jnp.float32),
            dma((n_col,)),
            dma((n_col,)),
            dma((ITERS, chunks, n_col)),
            dma((ITERS, chunks, n_col)),
            dma((ITERS, chunks, chips)),
            dma((ITERS, chunks, chips)),
            dma((ITERS, chunks, chips)),
            dma((ITERS, chunks, chips)),
        ],
        compiler_params=pltpu.CompilerParams(
            collective_id=0, has_side_effects=True, vmem_limit_bytes=56 * 2**20
        ),
    )(slot_of, tiles, cols[None, :], seed_node[None, :], teleport_block[None, :], previous)


def solution(mesh):
    in_specs = (
        P(("groups", "row"), "col", None, None, None),
        P(("groups", "row"), "col", None),
        P(("groups", "row"), "col", None),
        P("groups"),
        P("groups"),
        P(("groups", "row", "col"), None),
    )
    out_specs = P(("groups", "row", "col"), None)
    return jax.shard_map(
        on_device, mesh=mesh, in_specs=in_specs, out_specs=out_specs, check_vma=False
    )
```

```python
import functools

import jax
import jax.numpy as jnp
from jax import lax
from jax.experimental import pallas as pl
from jax.experimental.pallas import tpu as pltpu
from jax.sharding import PartitionSpec as P

ITERS = 3
LANES = 128
DAMPING = 0.85
MESH = pl.DeviceIdType.MESH


def refresh_kernel(
    n_row, n_col, slot_ref, tiles_ref, tile_col_ref, seed_ref, block_ref, prev_ref, out_ref,
    adj_ref, adj_sem, link, sums_out, sums_in, inverse, restart, panels, kept,
    pair_out, pair_in, half_out, half_in, full_out, full_in,
    sums_ss, sums_rs, col_ss, col_rs, pair_ss, pair_rs, row_ss, row_rs,
):
    r, c = lax.axis_index("row"), lax.axis_index("col")
    owned, seeds = prev_ref.shape
    slots, edge = adj_ref.shape[:2]
    held = owned // edge
    targets, sources = link.shape
    tile_rows, tile_cols = targets // edge, sources // edge
    chunks = seeds // LANES
    chips = n_row // 2
    chip, core = r // 2, lax.rem(r, 2)
    mate = r + 1 - 2 * core

    barrier = pltpu.get_barrier_semaphore()
    for d in range(1, n_col):
        pl.semaphore_signal(barrier, 1, device_id={"col": lax.rem(c + d, n_col)}, device_id_type=MESH)
    pl.semaphore_signal(barrier, 1, device_id={"row": mate}, device_id_type=MESH)
    for e in range(1, chips):
        pl.semaphore_signal(
            barrier, 1, device_id={"row": lax.rem(chip + e, chips) * 2 + core}, device_id_type=MESH
        )

    load = pltpu.make_async_copy(tiles_ref, adj_ref, adj_sem)
    load.start()
    row_of = lax.broadcasted_iota(jnp.int32, (owned, seeds), 0)
    first = (r * n_col + c) * owned
    at_seed = (row_of + first == seed_ref[...]).astype(jnp.float32)
    in_block = ((row_of + first) // edge == block_ref[...]).astype(jnp.float32)
    restart[...] = (1.0 - DAMPING) * (4.0 * at_seed + 2.0 * in_block)
    load.wait()

    tile_sums = jnp.sum(adj_ref[...].astype(jnp.float32), axis=1)
    column_of = lax.broadcasted_iota(jnp.int32, (tile_cols, slots), 0)
    placed = (column_of == tile_col_ref[...]).astype(jnp.float32)
    sums = jnp.dot(
        placed, tile_sums, precision=lax.Precision.HIGHEST, preferred_element_type=jnp.float32
    )
    for k in range(n_col):
        sums_out[k, :held] = sums[k * held : (k + 1) * held]

    pl.semaphore_wait(barrier, n_col - 1 + chips)

    def sums_copy(d):
        dst = lax.rem(c + d, n_col)
        return pltpu.make_async_remote_copy(
            src_ref=sums_out.at[dst], dst_ref=sums_in.at[d],
            send_sem=sums_ss.at[d], recv_sem=sums_rs.at[d],
            device_id={"col": dst}, device_id_type=MESH,
        )

    def col_copy(it, h, d):
        dst = lax.rem(c + d, n_col)
        place = panels.at[it, h, pl.ds(pl.multiple_of(c * owned, owned), owned)]
        return pltpu.make_async_remote_copy(
            src_ref=place, dst_ref=place,
            send_sem=col_ss.at[it, h, d], recv_sem=col_rs.at[it, h, d],
            device_id={"col": dst}, device_id_type=MESH,
        )

    def pair_copy(it, h, e):
        return pltpu.make_async_remote_copy(
            src_ref=pair_out.at[it, h, e], dst_ref=pair_in.at[it, h, e],
            send_sem=pair_ss.at[it, h, e], recv_sem=pair_rs.at[it, h, e],
            device_id={"row": mate}, device_id_type=MESH,
        )

    def row_copy(it, h, e):
        last = it == ITERS - 1
        src = full_out.at[h, e] if last else half_out.at[it, h, e]
        dst = full_in.at[h, e] if last else half_in.at[it, h, e]
        return pltpu.make_async_remote_copy(
            src_ref=src, dst_ref=dst,
            send_sem=row_ss.at[it, h, e], recv_sem=row_rs.at[it, h, e],
            device_id={"row": lax.rem(chip + e, chips) * 2 + core}, device_id_type=MESH,
        )

    def product(it, h, e, of_core):
        dst = lax.rem(chip + e, chips) * 2 + of_core
        rows = pl.ds(pl.multiple_of(dst * owned, owned), owned)
        return jnp.dot(link[rows, :], panels[it, h], preferred_element_type=jnp.float32)

    for d in range(1, n_col):
        sums_copy(d).start()

    @pl.loop(0, tile_rows)
    def _(i):
        for j in range(tile_cols):
            slot = slot_ref[i * tile_cols + j]
            tile = adj_ref[jnp.maximum(slot - 1, 0)]
            link[pl.ds(i * edge, edge), j * edge : (j + 1) * edge] = jnp.where(
                slot > 0, tile, jnp.zeros_like(tile)
            )

    total = sums_out[c, :held]
    for d in range(1, n_col):
        sums_copy(d).wait_recv()
        total = total + sums_in[d, :held]
    scale = 1.0 / jnp.maximum(total, 1.0)
    for t in range(held):
        wide = jnp.broadcast_to(scale[t : t + 1], (LANES, edge))
        inverse[t * edge : (t + 1) * edge] = jnp.transpose(wide)

    def share(it, h, ranks):
        place = pl.ds(pl.multiple_of(c * owned, owned), owned)
        panels[it, h, place] = (ranks * inverse[...]).astype(jnp.bfloat16)
        for d in range(1, n_col):
            col_copy(it, h, d).start()

    share(0, 0, prev_ref[:, :LANES])

    for it in range(ITERS):
        for h in range(chunks):
            for d in range(1, n_col):
                col_copy(it, h, d).wait_recv()
            @pl.loop(1, chips + 1, unroll=chips <= 2)
            def _(e):
                place = lax.rem(e, chips)
                pair_out[it, h, place] = product(it, h, place, 1 - core)
                pair_copy(it, h, place).start()

            @pl.loop(1, chips + 1, unroll=chips <= 2)
            def _(e):
                place = lax.rem(e, chips)
                kept[it, h, place] = product(it, h, place, core)

            if it == 0 and h + 1 < chunks:
                share(0, h + 1, prev_ref[:, (h + 1) * LANES : (h + 2) * LANES])
            for e in range(1, chips):
                pair_copy(it, h, e).wait_recv()
                part = kept[it, h, e] + pair_in[it, h, e]
                if it == ITERS - 1:
                    full_out[h, e] = part
                else:
                    half_out[it, h, e] = part.astype(jnp.bfloat16)
                row_copy(it, h, e).start()
            pair_copy(it, h, 0).wait_recv()
            summed = kept[it, h, 0] + pair_in[it, h, 0]
            for e in range(1, chips):
                row_copy(it, h, e).wait_recv()
                if it == ITERS - 1:
                    summed = summed + full_in[h, e]
                else:
                    summed = summed + half_in[it, h, e].astype(jnp.float32)
            lanes = slice(h * LANES, (h + 1) * LANES)
            ranks = DAMPING * summed + restart[:, lanes]
            if it == ITERS - 1:
                out_ref[:, lanes] = ranks
            else:
                share(it + 1, h, ranks)

    for d in range(1, n_col):
        sums_copy(d).wait_send()
    for it in range(ITERS):
        for h in range(chunks):
            for d in range(1, n_col):
                col_copy(it, h, d).wait_send()
            for e in range(chips):
                pair_copy(it, h, e).wait_send()
            for e in range(1, chips):
                row_copy(it, h, e).wait_send()


def on_device(adjacency, tile_row, tile_col, seed_node, teleport_block, previous):
    tiles = adjacency[0, 0]
    rows, cols = tile_row[0, 0], tile_col[0, 0]
    slots, edge = tiles.shape[:2]
    owned, seeds = previous.shape
    n_row, n_col = lax.axis_size("row"), lax.axis_size("col")
    targets, sources = n_row * owned, n_col * owned
    tile_rows, tile_cols = targets // edge, sources // edge
    chunks, chips = seeds // LANES, n_row // 2
    key = jnp.where(rows >= 0, rows * tile_cols + cols, -1)
    places = jnp.arange(tile_rows * tile_cols, dtype=jnp.int32)
    number = jnp.arange(1, slots + 1, dtype=jnp.int32)
    slot_of = jnp.sum(jnp.where(places[:, None] == key[None, :], number[None, :], 0), axis=1)
    vmem = pl.BlockSpec(memory_space=pltpu.VMEM)
    dma = pltpu.SemaphoreType.DMA
    return pl.pallas_call(
        functools.partial(refresh_kernel, n_row, n_col),
        out_shape=jax.ShapeDtypeStruct((owned, seeds), jnp.float32),
        in_specs=[pl.BlockSpec(memory_space=pltpu.SMEM), pl.BlockSpec(memory_space=pl.ANY)] + [vmem] * 4,
        out_specs=vmem,
        scratch_shapes=[
            pltpu.VMEM(tiles.shape, jnp.bfloat16),
            dma,
            pltpu.VMEM((targets, sources), jnp.bfloat16),
            pltpu.VMEM((n_col, 8, edge), jnp.float32),
            pltpu.VMEM((n_col, 8, edge), jnp.float32),
            pltpu.VMEM((owned, LANES), jnp.float32),
            pltpu.VMEM((owned, seeds), jnp.float32),
            pltpu.VMEM((ITERS, chunks, sources, LANES), jnp.bfloat16),
            pltpu.VMEM((ITERS, chunks, chips, owned, LANES), jnp.float32),
            pltpu.VMEM((ITERS, chunks, chips, owned, LANES), jnp.float32),
            pltpu.VMEM((ITERS, chunks, chips, owned, LANES), jnp.float32),
            pltpu.VMEM((ITERS - 1, chunks, chips, owned, LANES), jnp.bfloat16),
            pltpu.VMEM((ITERS - 1, chunks, chips, owned, LANES), jnp.bfloat16),
            pltpu.VMEM((chunks, chips, owned, LANES), jnp.float32),
            pltpu.VMEM((chunks, chips, owned, LANES), jnp.float32),
            dma((n_col,)),
            dma((n_col,)),
            dma((ITERS, chunks, n_col)),
            dma((ITERS, chunks, n_col)),
            dma((ITERS, chunks, chips)),
            dma((ITERS, chunks, chips)),
            dma((ITERS, chunks, chips)),
            dma((ITERS, chunks, chips)),
        ],
        compiler_params=pltpu.CompilerParams(
            collective_id=0, has_side_effects=True, vmem_limit_bytes=56 * 2**20
        ),
    )(slot_of, tiles, cols[None, :], seed_node[None, :], teleport_block[None, :], previous)


def solution(mesh):
    in_specs = (
        P(("groups", "row"), "col", None, None, None),
        P(("groups", "row"), "col", None),
        P(("groups", "row"), "col", None),
        P("groups"),
        P("groups"),
        P(("groups", "row", "col"), None),
    )
    out_specs = P(("groups", "row", "col"), None)
    return jax.shard_map(
        on_device, mesh=mesh, in_specs=in_specs, out_specs=out_specs, check_vma=False
    )
```
